512 devices in a mesh: grp: 32 (over x_hi, y, core), tp: 16 (over x_lo, z).
Axes of the slice: x: 4 (x_hi: 2, x_lo: 2; x = x_hi * 2 + x_lo), y: 8, z: 8, core: 2. Of those that a mesh axis runs over, the one named last changes fastest.
Arguments:
- hidden: bfloat16 [2048, 8192], P('grp'), may hold values from -6 to 6
- w_proj: bfloat16 [8192, 5120], P('grp', 'tp'), may hold values from -0.0625 to 0.0625
- cache_keys: bfloat16 [32, 2048, 512], P('grp', 'tp')
- cache_values: bfloat16 [32, 2048, 512], P('grp', 'tp'), may hold values from -24 to 24
- cand_issue: int32 [1024], P('grp'), may hold values from 0 to 31, as said below
- cand_length: int32 [1024], P('grp'), may hold values from 0 to 4, as said below
- prefix_len: int32 [32], P('grp'), may hold values from 256 to 2048, as said below
Outputs:
- attended: bfloat16 [2048, 4096], P('grp', 'tp')
The draws below stay inside these ranges and needn't reach their ends.
Inputs may be any that keep to these rules, and one draw needn't show every extreme that they name: `cand_length`: each anchor's 32 entries hold its candidates in order, then zeros; the lengths of one anchor sum to 64; every candidate but the last has 2 tokens or more, and the first has exactly 4. `cand_issue`: the candidates of one anchor name different issues; entries with length 0 are unused; issue i belongs to index i of grp. `prefix_len`: some issue has exactly 2048 cached positions.
All inputs are finite; a program needn't handle non-finite values.
Results may differ from the reference program's by a relative error of at most 0.012.
Values may be sent and summed in bfloat16 or wider, within the bound.
A program may use at most 64 MiB of HBM per device.

```python
import math
import jax
import jax.numpy as jnp
from jax import lax

D = 8192
HEADS = 32
KVH = 4
HD = 128
ROWS = 64
PREFIX = 2048
CAP = 4
SLOTS = 128
ROWS_ALL = 2048
PCOLS = 320
N_GRP = 32
N_TP = 16


def packing(key):
    key_len = jax.random.fold_in(key, 101)
    key_bias = jax.random.fold_in(key, 202)
    key_jitter = jax.random.fold_in(key, 303)
    half = CAP // 2
    raw = jax.random.randint(key_len, (N_GRP, N_GRP), half, CAP + 1)
    raw = raw.at[:, 0].set(CAP)
    ends = jnp.cumsum(raw, axis=1)
    starts = ends - raw
    length = jnp.clip(ROWS - starts, 0, raw)
    bias = jax.random.randint(key_bias, (1, N_GRP), 0, 2 * N_GRP)
    jitter = jax.random.randint(key_jitter, (N_GRP, N_GRP), 0, N_GRP)
    score = (bias + jitter) * N_GRP + jnp.arange(N_GRP)[None, :]
    order = jnp.argsort(-score, axis=1)
    return (length.reshape(-1).astype(jnp.int32), order.reshape(-1).astype(jnp.int32))


def draw_cand_length(key, part):
    return packing(key)[0]


def draw_cand_issue(key, part):
    return packing(key)[1]


def draw_prefix_len(key, part):
    lengths = jax.random.randint(jax.random.fold_in(key, 1), (N_GRP,), PREFIX // 8, PREFIX + 1)
    full = jax.random.randint(jax.random.fold_in(key, 2), (), 0, N_GRP)
    return jnp.where(jnp.arange(N_GRP) == full, PREFIX, lengths).astype(jnp.int32)


def draw_cache_keys(key, part):
    shape = (N_GRP, PREFIX, KVH * HD)
    base = jnp.clip(jax.random.normal(jax.random.fold_in(key, 5), shape, jnp.float32), -6.0, 6.0)
    scales = jnp.exp(jax.random.uniform(jax.random.fold_in(key, 6), (N_GRP, PREFIX, 1), jnp.float32, -0.7, 0.7))
    return (base * scales).astype(jnp.bfloat16)


def level_of(stream_key, shape, cuts, least, high):
    def one(dim, parts):
        steps = jax.random.uniform(jax.random.fold_in(jax.random.fold_in(stream_key, 6), dim), (parts,), jnp.float32, least / len(cuts), high / len(cuts))
        return jnp.repeat(jnp.exp(steps), shape[dim] // parts).reshape((-1,) + (1,) * (len(shape) - dim - 1))

    level = one(*cuts[0])
    for cut in cuts[1:]:
        level = level * one(*cut)
    return level


def scatter_about(own_key, dims, scale, bound, shards=(), kind=jnp.bfloat16):
    loudness = level_of(own_key, dims, shards, -0.22, 0.18) if shards else 1.0
    drawn = jax.random.normal(own_key, dims, jnp.float32) * scale * loudness
    return jnp.minimum(jnp.maximum(drawn, -bound), bound).astype(kind)


def setup_inputs(seed: int = 0) -> dict:
    key_list = jax.random.split(jax.random.key(seed), 8)
    hidden = scatter_about(key_list[0], (ROWS_ALL, D), 1.0, 6.0, ((0, 32),))
    w_proj = scatter_about(key_list[1], (D, N_TP * PCOLS), D ** -0.5, 0.0625, ((0, 32), (1, 16)))
    cache_keys = draw_cache_keys(jax.random.fold_in(key_list[7], 71), 0)
    cache_values = scatter_about(key_list[3], (N_GRP, PREFIX, KVH * HD), 4.0, 24.0, ((0, 32), (1, 16)))
    cand_issue = draw_cand_issue(jax.random.fold_in(key_list[7], 71), 0)
    cand_length = draw_cand_length(jax.random.fold_in(key_list[7], 71), 0)
    prefix_len = draw_prefix_len(jax.random.fold_in(key_list[7], 71), 0)
    return dict(hidden=hidden, w_proj=w_proj, cache_keys=cache_keys, cache_values=cache_values, cand_issue=cand_issue, cand_length=cand_length, prefix_len=prefix_len)


NEGATIVE = -1e+30
THETA = 1000000.0

def row_layout(cand_issue, cand_length, rows):
    ends = jnp.cumsum(cand_length).astype(jnp.int32)
    starts = (ends - cand_length).astype(jnp.int32)
    index = jnp.arange(rows).astype(jnp.int32)
    member = ((starts[None, :] <= index[:, None]) & (index[:, None] < ends[None, :])).astype(jnp.int32)
    issue = lax.optimization_barrier(jnp.sum(member * cand_issue[None, :], axis=1)).astype(jnp.int32)
    position = (index - lax.optimization_barrier(jnp.sum(member * starts[None, :], axis=1))).astype(jnp.int32)
    return (issue, position)

def rotary(values, positions):
    width = values.shape[-1]
    half = width // 2
    freq = THETA ** (-2.0 * jnp.arange(half).astype(jnp.float32) / width)
    angle = positions.astype(jnp.float32)[:, None] * freq[None, :]
    cosine = jnp.cos(angle)[:, None, :]
    sine = jnp.sin(angle)[:, None, :]
    first = values[..., :half]
    second = values[..., half:]
    return jnp.concatenate([first * cosine - second * sine, second * cosine + first * sine], axis=-1)

def reference(hidden, w_proj, cache_keys, cache_values, cand_issue, cand_length, prefix_len):
    groups = N_GRP
    cap = CAP
    slots = SLOTS
    group = HEADS // KVH
    q_cols = HEADS * HD // N_TP
    k_cols = KVH * HD // N_TP
    w_blocks = w_proj.reshape(D, N_TP, PCOLS)
    w_query = w_blocks[:, :, :q_cols].reshape(D, HEADS * HD)
    w_key = w_blocks[:, :, q_cols:q_cols + k_cols].reshape(D, KVH * HD)
    w_value = w_blocks[:, :, q_cols + k_cols:].reshape(D, KVH * HD)
    queries = jnp.dot(hidden, w_query, preferred_element_type=jnp.float32).astype(jnp.bfloat16)
    keys_new = jnp.dot(hidden, w_key, preferred_element_type=jnp.float32).astype(jnp.bfloat16)
    values_new = jnp.dot(hidden, w_value, preferred_element_type=jnp.float32).astype(jnp.bfloat16)
    issue, position = jax.vmap(lambda first, second: row_layout(first, second, ROWS))(cand_issue.reshape(groups, groups), cand_length.reshape(groups, groups))
    anchor = jnp.broadcast_to(jnp.arange(groups).astype(jnp.int32)[:, None], (groups, ROWS))
    slot = (issue * slots + anchor * cap + position).reshape(-1).astype(jnp.int32)
    counts = jnp.zeros((groups, groups), jnp.int32).at[issue.reshape(-1), anchor.reshape(-1)].add(1)

    def place(values):
        filled = jnp.zeros((groups * slots, values.shape[1]), values.dtype).at[slot].set(values)
        return filled.reshape(groups, slots, values.shape[1])
    slot_index = jnp.arange(slots).astype(jnp.int32)
    slot_anchor = slot_index // cap
    slot_within = slot_index % cap
    scale = 1.0 / math.sqrt(HD)

    def attend(items):
        q_i, k_i, v_i, count_i, length_i, keys_i, values_i = items
        positions = length_i + slot_within
        q_rot = rotary(q_i.astype(jnp.float32).reshape(slots, HEADS, HD), positions).astype(jnp.bfloat16)
        k_rot = rotary(k_i.astype(jnp.float32).reshape(slots, KVH, HD), positions).astype(jnp.bfloat16)
        limit = count_i[slot_anchor]
        own = (slot_anchor[:, None] == slot_anchor[None, :]) & (slot_within[None, :] <= slot_within[:, None])
        own = own & (slot_within[None, :] < limit[None, :])
        own = jnp.repeat(own, group, axis=0)
        early = (jnp.arange(PREFIX).astype(jnp.int32) < length_i)[None, :]
        pieces = []
        for head in range(KVH):
            query = q_rot[:, head * group:(head + 1) * group, :].reshape(slots * group, HD)
            cached_k = keys_i[:, head * HD:(head + 1) * HD]
            cached_v = values_i[:, head * HD:(head + 1) * HD]
            score_p = jnp.where(early, jnp.dot(query, cached_k.T, preferred_element_type=jnp.float32) * scale, NEGATIVE)
            score_o = jnp.where(own, jnp.dot(query, k_rot[:, head, :].T, preferred_element_type=jnp.float32) * scale, NEGATIVE)
            top = jnp.maximum(lax.optimization_barrier(jnp.max(score_p, axis=1)), lax.optimization_barrier(jnp.max(score_o, axis=1)))
            w_p = jnp.where(early, jnp.exp(score_p - top[:, None]), 0.0)
            w_o = jnp.where(own, jnp.exp(score_o - top[:, None]), 0.0)
            total = lax.optimization_barrier(jnp.sum(w_p, axis=1)) + lax.optimization_barrier(jnp.sum(w_o, axis=1))
            mixed = jnp.dot(w_p.astype(jnp.bfloat16), cached_v, preferred_element_type=jnp.float32)
            mixed = mixed + jnp.dot(w_o.astype(jnp.bfloat16), v_i[:, head * HD:(head + 1) * HD], preferred_element_type=jnp.float32)
            pieces.append((mixed / total[:, None]).reshape(slots, group * HD))
        return jnp.concatenate(pieces, axis=1).astype(jnp.bfloat16)
    attended = lax.map(attend, (place(queries), place(keys_new), place(values_new), counts, prefix_len, cache_keys, cache_values))
    return attended.reshape(groups * slots, HEADS * HD)[slot]
```

```python
import functools
import math

import jax
import jax.numpy as jnp
import numpy as np
from jax import lax
from jax.experimental import pallas as pl
from jax.experimental.pallas import tpu as pltpu
from jax.sharding import PartitionSpec as P

HD = 128
NEGATIVE = -1e30
THETA = 1000000.0
CAP = 4
F32 = jnp.float32
BF16 = jnp.bfloat16


def iota(shape, axis):
    return lax.broadcasted_iota(jnp.int32, shape, axis)


def nt(left, right):
    return lax.dot_general(left, right, (((1,), (1,)), ((), ())), preferred_element_type=F32)


def nn(left, right):
    return jnp.dot(left, right, preferred_element_type=F32)


def rotated(values, cosine, sine):
    return values * cosine + pltpu.roll(values, HD // 2, 1) * sine


def kernel(
    groups, ranks,
    hid_hbm, w_hbm, ck_hbm, cv_hbm, issue_ref, length_ref, prefix_ref, freq_ref,
    out_ref,
    hid, wbuf, kbuf, vbuf, acc, qs, qr, kvs, kvx, rs, rr,
    load_sem, w_send, w_x, w_ring, w_sib, c_send, c_recv, q_sem, kv_send, kv_recv, r_sem,
):
    g = lax.axis_index("grp")
    t = lax.axis_index("tp")
    x_hi = g // 16
    y = (g // 2) % 8
    core = g % 2
    block = ck_hbm.shape[1]
    rows = hid.shape[0]
    depth = w_hbm.shape[1]
    cols = w_hbm.shape[0]
    half = cols // 2

    def place(xx, yy, cc):
        return xx * 16 + lax.rem(yy + 8, 8) * 2 + cc

    right = place(x_hi, y + 1, core)
    left = place(x_hi, y - 1, core)
    partner = place(1 - x_hi, y, core)
    sibling = place(x_hi, y, 1 - core)

    load_hid = pltpu.make_async_copy(hid_hbm, hid, load_sem.at[0])
    load_hid.start()
    load_w = pltpu.make_async_copy(w_hbm, wbuf.at[g], load_sem.at[1])
    load_w.start()
    my_head = pl.multiple_of((t // 4) * HD, HD)
    my_rows = pl.ds(pl.multiple_of(t * block, block), block)
    load_k = pltpu.make_async_copy(ck_hbm.at[0, :, pl.ds(my_head, HD)], kbuf.at[my_rows], load_sem.at[2])
    load_k.start()
    load_v = pltpu.make_async_copy(cv_hbm.at[0, :, pl.ds(my_head, HD)], vbuf.at[my_rows], load_sem.at[3])
    load_v.start()

    barrier = pltpu.get_barrier_semaphore()

    def greet_grp(step, carry):
        pl.semaphore_signal(barrier, inc=1, device_id={"grp": lax.rem(g + step, groups)},
                            device_id_type=pl.DeviceIdType.MESH)
        return carry

    def greet_tp(step, carry):
        pl.semaphore_signal(barrier, inc=1, device_id={"tp": lax.rem(t + step, ranks)},
                            device_id_type=pl.DeviceIdType.MESH)
        return carry

    lax.fori_loop(1, groups, greet_grp, 0)
    lax.fori_loop(1, ranks, greet_tp, 0)
    pl.semaphore_wait(barrier, groups + ranks - 2)

    sends = []

    def push(source, index, part, arrived, target):
        copy = pltpu.make_async_remote_copy(
            src_ref=source, dst_ref=wbuf.at[index] if part is None else wbuf.at[index, part],
            send_sem=w_send.at[len(sends)], recv_sem=arrived,
            device_id={"grp": target}, device_id_type=pl.DeviceIdType.MESH)
        copy.start()
        sends.append(copy)

    def pull(index, part, arrived):
        where = wbuf.at[index] if part is None else wbuf.at[index, part]
        pltpu.make_async_remote_copy(
            src_ref=where, dst_ref=where, send_sem=w_send.at[0], recv_sem=arrived,
            device_id={"grp": sibling}, device_id_type=pl.DeviceIdType.MESH).wait_recv()

    def ring(line, way, hop):
        return w_ring.at[line * 8 + way * 4 + hop - 1]

    def sib(line, kind):
        return w_sib.at[line * 9 + kind]

    push(w_hbm, g, None, w_x.at[0], partner)
    push(w_hbm, g, None, ring(0, 0, 1), right)
    push(w_hbm, g, None, ring(0, 1, 1), left)
    push(w_hbm, g, None, sib(0, 0), sibling)

    def cache_copy(step, which):
        other = lax.rem(t + step, ranks)
        head = pl.ds(pl.multiple_of((other // 4) * HD, HD), HD)
        source, dest = ((ck_hbm, kbuf), (cv_hbm, vbuf))[which]
        return pltpu.make_async_remote_copy(
            src_ref=source.at[0, :, head], dst_ref=dest.at[my_rows],
            send_sem=c_send.at[which], recv_sem=c_recv.at[which],
            device_id={"tp": other}, device_id_type=pl.DeviceIdType.MESH)

    def send_cache(step, carry):
        cache_copy(step, 0).start()
        cache_copy(step, 1).start()
        return carry

    lax.fori_loop(1, ranks, send_cache, 0)

    lane = iota((1, 2 * rows), 1) & (rows - 1)
    down = iota((rows, 1), 0)
    issue_l = jnp.zeros((1, 2 * rows), jnp.int32)
    start_l = jnp.zeros((1, 2 * rows), jnp.int32)
    issue_d = jnp.zeros((rows, 1), jnp.int32)
    start_d = jnp.zeros((rows, 1), jnp.int32)
    begin = jnp.int32(0)
    for entry in range(issue_ref.shape[0]):
        end = begin + length_ref[entry]
        name = issue_ref[entry]
        in_l = (lane >= begin) & (lane < end)
        in_d = (down >= begin) & (down < end)
        issue_l = jnp.where(in_l, name, issue_l)
        start_l = jnp.where(in_l, begin, start_l)
        issue_d = jnp.where(in_d, name, issue_d)
        start_d = jnp.where(in_d, begin, start_d)
        begin = end
    pos_l = lane - start_l
    pos_d = down - start_d
    slot_l = issue_l * CAP + pos_l
    slot_d = issue_d * CAP + pos_d

    prefix = prefix_ref[0]
    sign = jnp.where(iota((1, HD), 1) < HD // 2, -1.0, 1.0).astype(F32)
    freq = freq_ref[0:1, :]
    angle_q = (prefix + (iota((8, 1), 0) & 3)).astype(F32) * freq
    cos_q = jnp.cos(angle_q)
    sin_q = jnp.sin(angle_q) * sign
    angle_o = pos_d.astype(F32) * freq
    cos_o = jnp.cos(angle_o)
    sin_o = jnp.sin(angle_o) * sign

    def mac(index):
        part = pl.ds(pl.multiple_of(index * depth, depth), depth)
        acc[...] += nt(hid[:, part], wbuf[index])

    acc[...] = jnp.zeros_like(acc)
    load_hid.wait()
    load_w.wait()
    mac(g)

    low, high = pl.ds(0, half), pl.ds(half, half)
    where_x = (x_hi, 1 - x_hi)

    def from_sibling(line, hop):
        if hop == 0:
            index = place(where_x[line], y, 1 - core)
            pull(index, None, sib(line, 0))
            mac(index)
        elif hop < 4:
            for way, yy in ((0, y - hop), (1, y + hop)):
                index = place(where_x[line], yy, 1 - core)
                pull(index, None, sib(line, 1 + way * 4 + hop - 1))
                mac(index)
        else:
            index = place(where_x[line], y + 4, 1 - core)
            pull(index, low, sib(line, 4))
            pull(index, high, sib(line, 8))
            mac(index)

    def from_ring(line, hop):
        if hop < 4:
            indices = []
            for way, yy, nxt, part in ((0, y - hop, right, low), (1, y + hop, left, high)):
                index = place(where_x[line], yy, core)
                pull(index, None, ring(line, way, hop))
                if hop < 3:
                    push(wbuf.at[index], index, None, ring(line, way, hop + 1), nxt)
                else:
                    push(wbuf.at[index, part], index, part, ring(line, way, 4), nxt)
                push(wbuf.at[index], index, None, sib(line, 1 + way * 4 + hop - 1), sibling)
                indices.append(index)
            for index in indices:
                mac(index)
        else:
            index = place(where_x[line], y + 4, core)
            for way, part in ((0, low), (1, high)):
                pull(index, part, ring(line, way, 4))
                push(wbuf.at[index, part], index, part, sib(line, 4 + way * 4), sibling)
            mac(index)

    def from_partner():
        pull(partner, None, w_x.at[0])
        push(wbuf.at[partner], partner, None, ring(1, 0, 1), right)
        push(wbuf.at[partner], partner, None, ring(1, 1, 1), left)
        push(wbuf.at[partner], partner, None, sib(1, 0), sibling)
        mac(partner)

    from_sibling(0, 0)
    from_ring(0, 1)
    from_partner()
    from_ring(0, 2)
    from_sibling(0, 1)
    from_sibling(1, 0)
    from_ring(1, 1)
    from_ring(0, 3)
    from_sibling(0, 2)
    from_ring(1, 2)
    from_sibling(1, 1)
    from_ring(0, 4)
    from_sibling(0, 3)
    from_ring(1, 3)
    from_sibling(1, 2)
    from_sibling(0, 4)
    from_ring(1, 4)
    from_sibling(1, 3)
    from_sibling(1, 4)

    proj = acc[...].astype(BF16)
    stacked = jnp.concatenate([proj[:, :HD], proj[:, HD:2 * HD]], axis=0)
    row = iota((8 * groups, 2 * rows), 0)
    pick = ((row >> 3) * CAP + (row & 3) == slot_l) & (
        ((row >> 2) & 1) == (iota((8 * groups, 2 * rows), 1) >= rows).astype(jnp.int32))
    qs[...] = nn(pick.astype(F32).astype(BF16), stacked)

    my_q = pl.ds(pl.multiple_of(g * 8, 8), 8)

    def q_copy(step):
        other = lax.rem(g + step, groups)
        return pltpu.make_async_remote_copy(
            src_ref=qs.at[pl.ds(pl.multiple_of(other * 8, 8), 8)], dst_ref=qr.at[my_q],
            send_sem=q_sem.at[0], recv_sem=q_sem.at[1],
            device_id={"grp": other}, device_id_type=pl.DeviceIdType.MESH)

    def send_q(step, carry):
        q_copy(step).start()
        return carry

    lax.fori_loop(1, groups, send_q, 0)
    qr[my_q, :] = qs[my_q, :]

    kvs[...] = jnp.concatenate([proj[:, 2 * HD:], jnp.zeros((rows, 2 * HD - (cols - 2 * HD) - HD), BF16)], axis=1)
    base = (t // 4) * 4
    kv_copies = []
    for step in (1, 2, 3):
        other = base + lax.rem(t + step, 4)
        copy = pltpu.make_async_remote_copy(
            src_ref=kvs, dst_ref=kvx.at[lax.rem(t, 4)],
            send_sem=kv_send.at[step], recv_sem=kv_recv.at[lax.rem(t, 4)],
            device_id={"tp": other}, device_id_type=pl.DeviceIdType.MESH)
        copy.start()
        kv_copies.append(copy)
    kvx[lax.rem(t, 4)] = kvs[...]

    load_k.wait()
    load_v.wait()
    rest = pl.ds(0, block * (ranks - 1))
    for which, dest in ((0, kbuf), (1, vbuf)):
        pltpu.make_async_remote_copy(
            src_ref=dest.at[rest], dst_ref=dest.at[rest], send_sem=c_send.at[which], recv_sem=c_recv.at[which],
            device_id={"grp": sibling}, device_id_type=pl.DeviceIdType.MESH).wait()
    rest_q = pl.ds(0, 8 * (groups - 1))
    pltpu.make_async_remote_copy(
        src_ref=qs.at[rest_q], dst_ref=qr.at[rest_q], send_sem=q_sem.at[0], recv_sem=q_sem.at[1],
        device_id={"grp": sibling}, device_id_type=pl.DeviceIdType.MESH).wait()

    scale = 1.0 / math.sqrt(HD)
    tall = 8 * groups
    full = (groups, 8, HD)
    query = rotated(qr[...], jnp.broadcast_to(cos_q[None], full).reshape(tall, HD),
                    jnp.broadcast_to(sin_q[None], full).reshape(tall, HD)).astype(BF16)
    score = nt(query, kbuf[...])
    early = iota((1, block * ranks), 1) < prefix
    score = jnp.where(early, score * scale, NEGATIVE)
    top = jnp.max(score, axis=1, keepdims=True)
    weight = jnp.exp(score - top)
    total = jnp.sum(weight, axis=1, keepdims=True)
    mixed = nn(weight.astype(BF16), vbuf[...]) / total
    level = jnp.broadcast_to(top + jnp.log(total), (tall, HD))
    hi = level.astype(BF16).astype(F32)
    mid = (level - hi).astype(BF16).astype(F32)
    lo = level - hi - mid
    across = iota((tall, HD), 1)
    stats = jnp.where(across < 32, hi, jnp.where(across < 64, mid, lo))
    rs[...] = jnp.concatenate([mixed.reshape(full), stats.reshape(full)], axis=1).astype(BF16)

    def r_copy(step):
        other = lax.rem(g + step, groups)
        return pltpu.make_async_remote_copy(
            src_ref=rs.at[other], dst_ref=rr.at[g],
            send_sem=r_sem.at[0], recv_sem=r_sem.at[1],
            device_id={"grp": other}, device_id_type=pl.DeviceIdType.MESH)

    def send_r(step, carry):
        r_copy(step).start()
        return carry

    lax.fori_loop(1, groups, send_r, 0)
    rr[g] = rs[g]

    for step in (1, 2, 3):
        source = lax.rem(t + step, 4)
        pltpu.make_async_remote_copy(
            src_ref=kvs, dst_ref=kvx.at[source], send_sem=kv_send.at[step], recv_sem=kv_recv.at[source],
            device_id={"grp": sibling}, device_id_type=pl.DeviceIdType.MESH).wait_recv()
    wide = jnp.concatenate([kvx[0], kvx[1], kvx[2], kvx[3]], axis=1)
    a = iota((4 * HD, 2 * HD), 0)
    b = iota((4 * HD, 2 * HD), 1)
    lane_a = a & (HD - 1)
    goal = (lane_a >> 5) * HD + (a >> 7) * 32 + (lane_a & 31)
    spread = ((goal == b) & (lane_a < 64)).astype(F32).astype(BF16)
    both = nn(wide, spread)
    keys = rotated(both[:, :HD], cos_o, sin_o).astype(BF16)
    values = both[:, HD:].astype(BF16)
    same = (issue_d == issue_l[:, :rows]) & (pos_l[:, :rows] <= pos_d)
    own = []
    for head in range(2):
        mine = rotated(proj[:, head * HD:(head + 1) * HD].astype(F32), cos_o, sin_o).astype(BF16)
        part = jnp.where(same, nt(mine, keys) * scale, NEGATIVE)
        peak = jnp.max(part, axis=1, keepdims=True)
        share = jnp.where(same, jnp.exp(part - peak), 0.0)
        own.append((peak, jnp.sum(share, axis=1, keepdims=True), nn(share.astype(BF16), values)))

    big = 16 * groups
    r = iota((rows, big), 1)
    hit = (r >> 4) * CAP + (r & 3) == slot_d
    field = (r >> 2) & 3
    picks = [(hit & (field == kind)).astype(F32).astype(BF16) for kind in range(4)]

    rest_r = pl.ds(0, groups - 1)
    pltpu.make_async_remote_copy(
        src_ref=rs.at[rest_r], dst_ref=rr.at[rest_r], send_sem=r_sem.at[0], recv_sem=r_sem.at[1],
        device_id={"grp": sibling}, device_id_type=pl.DeviceIdType.MESH).wait()
    back = rr[...].reshape(big, HD)
    for head in range(2):
        cached = nn(picks[head], back)
        told = nn(picks[2 + head], back)
        log_c = told[:, 0:1] + told[:, 32:33] + told[:, 64:65]
        peak, total_o, mixed_o = own[head]
        summit = jnp.maximum(peak, log_c)
        part_o = jnp.exp(peak - summit)
        part_c = jnp.exp(log_c - summit)
        value = (mixed_o * part_o + cached * part_c) / (total_o * part_o + part_c)
        out_ref[:, head * HD:(head + 1) * HD] = value.astype(BF16)

    for copy in kv_copies:
        copy.wait_send()
    for copy in sends:
        copy.wait_send()


def local(groups, ranks, hidden, w_proj, cache_keys, cache_values, cand_issue, cand_length, prefix_len):
    rows, model = hidden.shape
    depth, cols = w_proj.shape
    block = cache_keys.shape[1]
    spot = np.arange(HD) % (HD // 2)
    freq = np.broadcast_to((THETA ** (-2.0 * spot / HD)).astype(np.float32), (8, HD))
    any_space = pl.BlockSpec(memory_space=pl.ANY)
    smem = pl.BlockSpec(memory_space=pltpu.SMEM)
    vmem = pl.BlockSpec(memory_space=pltpu.VMEM)
    dma = pltpu.SemaphoreType.DMA
    return pl.pallas_call(
        functools.partial(kernel, groups, ranks),
        out_shape=jax.ShapeDtypeStruct((rows, 2 * HD), BF16),
        in_specs=[any_space] * 4 + [smem] * 3 + [vmem],
        out_specs=vmem,
        scratch_shapes=[
            pltpu.VMEM((rows, model), BF16),
            pltpu.VMEM((groups, cols, depth), BF16),
            pltpu.VMEM((block * ranks, HD), BF16),
            pltpu.VMEM((block * ranks, HD), BF16),
            pltpu.VMEM((rows, cols), F32),
            pltpu.VMEM((8 * groups, HD), F32),
            pltpu.VMEM((8 * groups, HD), F32),
            pltpu.VMEM((rows, HD), BF16),
            pltpu.VMEM((4, rows, HD), BF16),
            pltpu.VMEM((groups, 16, HD), BF16),
            pltpu.VMEM((groups, 16, HD), BF16),
            dma((4,)), dma((40,)), dma((1,)), dma((16,)), dma((18,)), dma((2,)), dma((2,)), dma((2,)),
            dma((4,)), dma((4,)), dma((2,)),
        ],
        compiler_params=pltpu.CompilerParams(
            collective_id=0, has_side_effects=True, vmem_limit_bytes=48 * 1024 * 1024),
        cost_estimate=pl.CostEstimate(flops=10**9, bytes_accessed=2 * 10**6, transcendentals=10**6),
    )(hidden, w_proj.T, cache_keys, cache_values, cand_issue, cand_length, prefix_len, jnp.asarray(freq))


def solution(mesh):
    placed = (
        P("grp", None),
        P("grp", "tp"),
        P("grp", "tp", None),
        P("grp", "tp", None),
        P("grp"),
        P("grp"),
        P("grp"),
    )
    return jax.shard_map(
        functools.partial(local, mesh.shape["grp"], mesh.shape["tp"]),
        mesh=mesh, in_specs=placed, out_specs=P("grp", "tp"), check_vma=False)
```

```python
import functools
import math

import jax
import jax.numpy as jnp
import numpy as np
from jax import lax
from jax.experimental import pallas as pl
from jax.experimental.pallas import tpu as pltpu
from jax.sharding import PartitionSpec as P

HD = 128
NEGATIVE = -1e30
THETA = 1000000.0
CAP = 4
F32 = jnp.float32
BF16 = jnp.bfloat16


def iota(shape, axis):
    return lax.broadcasted_iota(jnp.int32, shape, axis)


def nt(left, right):
    return lax.dot_general(left, right, (((1,), (1,)), ((), ())), preferred_element_type=F32)


def nn(left, right):
    return jnp.dot(left, right, preferred_element_type=F32)


def rotated(values, cosine, sine):
    return values * cosine + pltpu.roll(values, HD // 2, 1) * sine


def kernel(
    groups, ranks,
    hid_hbm, w_hbm, ck_hbm, cv_hbm, issue_ref, length_ref, prefix_ref, freq_ref,
    out_ref,
    hid, wbuf, kbuf, vbuf, acc, px, qs, qr, kvs, kvx, rs, rr,
    load_sem, w_send, w_ring, w_sib, h_send, h_recv, p_sem, c_send, c_recv, q_sem, kv_send, kv_recv, r_sem,
):
    g = lax.axis_index("grp")
    t = lax.axis_index("tp")
    x_hi = g // 16
    y = (g // 2) % 8
    core = g % 2
    block = ck_hbm.shape[1]
    rows = hid_hbm.shape[0]
    span = hid_hbm.shape[1] // 2
    depth = w_hbm.shape[1]
    cols = w_hbm.shape[0]
    half = cols // 2

    def place(xx, yy, cc):
        return xx * 16 + lax.rem(yy + 8, 8) * 2 + cc

    right = place(x_hi, y + 1, core)
    left = place(x_hi, y - 1, core)
    partner = place(1 - x_hi, y, core)
    sibling = place(x_hi, y, 1 - core)

    my_span = pl.ds(pl.multiple_of(x_hi * span, span), span)
    load_hid = pltpu.make_async_copy(hid_hbm.at[:, my_span], hid.at[0:rows], load_sem.at[0])
    load_hid.start()
    load_w = pltpu.make_async_copy(w_hbm, wbuf.at[lax.rem(g, 16)], load_sem.at[1])
    load_w.start()
    my_head = pl.multiple_of((t // 4) * HD, HD)
    my_rows = pl.ds(pl.multiple_of(t * block, block), block)
    load_k = pltpu.make_async_copy(ck_hbm.at[0, :, pl.ds(my_head, HD)], kbuf.at[my_rows], load_sem.at[2])
    load_k.start()
    load_v = pltpu.make_async_copy(cv_hbm.at[0, :, pl.ds(my_head, HD)], vbuf.at[my_rows], load_sem.at[3])
    load_v.start()

    barrier = pltpu.get_barrier_semaphore()

    def greet_grp(step, carry):
        pl.semaphore_signal(barrier, inc=1, device_id={"grp": lax.rem(g + step, groups)},
                            device_id_type=pl.DeviceIdType.MESH)
        return carry

    def greet_tp(step, carry):
        pl.semaphore_signal(barrier, inc=1, device_id={"tp": lax.rem(t + step, ranks)},
                            device_id_type=pl.DeviceIdType.MESH)
        return carry

    lax.fori_loop(1, groups, greet_grp, 0)
    lax.fori_loop(1, ranks, greet_tp, 0)
    pl.semaphore_signal(barrier, inc=1, device_id={"grp": partner, "tp": lax.rem(t + 8, ranks)},
                        device_id_type=pl.DeviceIdType.MESH)
    pl.semaphore_wait(barrier, groups + ranks - 1)

    sends = []

    def push(source, index, part, arrived, target):
        copy = pltpu.make_async_remote_copy(
            src_ref=source, dst_ref=wbuf.at[index] if part is None else wbuf.at[index, part],
            send_sem=w_send.at[len(sends)], recv_sem=arrived,
            device_id={"grp": target}, device_id_type=pl.DeviceIdType.MESH)
        copy.start()
        sends.append(copy)

    def pull(index, part, arrived):
        where = wbuf.at[index] if part is None else wbuf.at[index, part]
        pltpu.make_async_remote_copy(
            src_ref=where, dst_ref=where, send_sem=w_send.at[0], recv_sem=arrived,
            device_id={"grp": sibling}, device_id_type=pl.DeviceIdType.MESH).wait_recv()

    def ring(way, hop):
        return w_ring.at[way * 4 + hop - 1]

    def line(yy, cc):
        return lax.rem(yy + 8, 8) * 2 + cc

    mine = line(y, core)
    push(w_hbm, mine, None, ring(0, 1), right)
    push(w_hbm, mine, None, ring(1, 1), left)
    push(w_hbm, mine, None, w_sib.at[0], sibling)

    def hid_copy(order, yy):
        far = pl.ds(pl.multiple_of((1 - x_hi) * span + lax.rem(yy + 8, 8) * 2 * depth, 2 * depth), 2 * depth)
        near = pl.ds(pl.multiple_of(lax.rem(yy + 8, 8) * 2 * depth, 2 * depth), 2 * depth)
        return pltpu.make_async_remote_copy(
            src_ref=hid_hbm.at[:, far], dst_ref=hid.at[rows:2 * rows, near],
            send_sem=h_send.at[order], recv_sem=h_recv.at[order],
            device_id={"grp": partner, "tp": lax.rem(t + 8, ranks)}, device_id_type=pl.DeviceIdType.MESH)

    hid_copies = [hid_copy(order, y + step) for order, step in enumerate((0, -1, 1, -2, 2, -3, 3, 4))]
    for copy in hid_copies:
        copy.start()

    def cache_copy(step, which):
        other = lax.rem(t + step, ranks)
        head = pl.ds(pl.multiple_of((other // 4) * HD, HD), HD)
        source, dest = ((ck_hbm, kbuf), (cv_hbm, vbuf))[which]
        return pltpu.make_async_remote_copy(
            src_ref=source.at[0, :, head], dst_ref=dest.at[my_rows],
            send_sem=c_send.at[which], recv_sem=c_recv.at[which],
            device_id={"tp": other}, device_id_type=pl.DeviceIdType.MESH)

    def send_cache(step, carry):
        cache_copy(step, 0).start()
        cache_copy(step, 1).start()
        return carry

    lax.fori_loop(1, ranks, send_cache, 0)

    lane = iota((1, 2 * rows), 1) & (rows - 1)
    down = iota((rows, 1), 0)
    issue_l = jnp.zeros((1, 2 * rows), jnp.int32)
    start_l = jnp.zeros((1, 2 * rows), jnp.int32)
    issue_d = jnp.zeros((rows, 1), jnp.int32)
    start_d = jnp.zeros((rows, 1), jnp.int32)
    begin = jnp.int32(0)
    for entry in range(issue_ref.shape[0]):
        end = begin + length_ref[entry]
        name = issue_ref[entry]
        in_l = (lane >= begin) & (lane < end)
        in_d = (down >= begin) & (down < end)
        issue_l = jnp.where(in_l, name, issue_l)
        start_l = jnp.where(in_l, begin, start_l)
        issue_d = jnp.where(in_d, name, issue_d)
        start_d = jnp.where(in_d, begin, start_d)
        begin = end
    pos_l = lane - start_l
    pos_d = down - start_d
    slot_l = issue_l * CAP + pos_l
    slot_d = issue_d * CAP + pos_d

    prefix = prefix_ref[0]
    sign = jnp.where(iota((1, HD), 1) < HD // 2, -1.0, 1.0).astype(F32)
    freq = freq_ref[0:1, :]
    angle_q = (prefix + (iota((8, 1), 0) & 3)).astype(F32) * freq
    cos_q = jnp.cos(angle_q)
    sin_q = jnp.sin(angle_q) * sign
    angle_o = pos_d.astype(F32) * freq
    cos_o = jnp.cos(angle_o)
    sin_o = jnp.sin(angle_o) * sign

    def mac(index):
        part = pl.ds(pl.multiple_of(index * depth, depth), depth)
        acc[...] += nt(hid[:, part], wbuf[index])

    acc[...] = jnp.zeros_like(acc)
    load_hid.wait()
    load_w.wait()
    hid_copies[0].wait_recv()
    mac(mine)

    low, high = pl.ds(0, half), pl.ds(half, half)

    def from_sibling(hop):
        if hop == 0:
            index = line(y, 1 - core)
            pull(index, None, w_sib.at[0])
            mac(index)
        elif hop < 4:
            for way, yy in ((0, y - hop), (1, y + hop)):
                index = line(yy, 1 - core)
                pull(index, None, w_sib.at[1 + way * 4 + hop - 1])
                mac(index)
        else:
            index = line(y + 4, 1 - core)
            pull(index, low, w_sib.at[4])
            pull(index, high, w_sib.at[8])
            mac(index)

    def from_ring(hop):
        if hop < 4:
            indices = []
            for way, yy, nxt, part in ((0, y - hop, right, low), (1, y + hop, left, high)):
                index = line(yy, core)
                pull(index, None, ring(way, hop))
                if hop < 3:
                    push(wbuf.at[index], index, None, ring(way, hop + 1), nxt)
                else:
                    push(wbuf.at[index, part], index, part, ring(way, 4), nxt)
                push(wbuf.at[index], index, None, w_sib.at[1 + way * 4 + hop - 1], sibling)
                indices.append(index)
            for way, index in enumerate(indices):
                hid_copies[hop * 2 - 1 + way].wait_recv()
                mac(index)
        else:
            index = line(y + 4, core)
            for way, part in ((0, low), (1, high)):
                pull(index, part, ring(way, 4))
                push(wbuf.at[index, part], index, part, w_sib.at[4 + way * 4], sibling)
            hid_copies[7].wait_recv()
            mac(index)

    from_sibling(0)
    from_ring(1)
    from_sibling(1)
    from_ring(2)
    from_sibling(2)
    from_ring(3)
    from_sibling(3)
    from_ring(4)
    from_sibling(4)

    swap = pltpu.make_async_remote_copy(
        src_ref=acc.at[rows:2 * rows], dst_ref=px, send_sem=p_sem.at[0], recv_sem=p_sem.at[1],
        device_id={"grp": partner}, device_id_type=pl.DeviceIdType.MESH)
    swap.start()
    swap.wait_recv()

    proj = (acc[0:rows, :] + px[...]).astype(BF16)
    stacked = jnp.concatenate([proj[:, :HD], proj[:, HD:2 * HD]], axis=0)
    row = iota((8 * groups, 2 * rows), 0)
    pick = ((row >> 3) * CAP + (row & 3) == slot_l) & (
        ((row >> 2) & 1) == (iota((8 * groups, 2 * rows), 1) >= rows).astype(jnp.int32))
    qs[...] = nn(pick.astype(F32).astype(BF16), stacked)

    my_q = pl.ds(pl.multiple_of(g * 8, 8), 8)

    def q_copy(step):
        other = lax.rem(g + step, groups)
        return pltpu.make_async_remote_copy(
            src_ref=qs.at[pl.ds(pl.multiple_of(other * 8, 8), 8)], dst_ref=qr.at[my_q],
            send_sem=q_sem.at[0], recv_sem=q_sem.at[1],
            device_id={"grp": other}, device_id_type=pl.DeviceIdType.MESH)

    def send_q(step, carry):
        q_copy(step).start()
        return carry

    lax.fori_loop(1, groups, send_q, 0)
    qr[my_q, :] = qs[my_q, :]

    kvs[...] = jnp.concatenate([proj[:, 2 * HD:], jnp.zeros((rows, 2 * HD - (cols - 2 * HD) - HD), BF16)], axis=1)
    base = (t // 4) * 4
    kv_copies = []
    for step in (1, 2, 3):
        other = base + lax.rem(t + step, 4)
        copy = pltpu.make_async_remote_copy(
            src_ref=kvs, dst_ref=kvx.at[lax.rem(t, 4)],
            send_sem=kv_send.at[step], recv_sem=kv_recv.at[lax.rem(t, 4)],
            device_id={"tp": other}, device_id_type=pl.DeviceIdType.MESH)
        copy.start()
        kv_copies.append(copy)
    kvx[lax.rem(t, 4)] = kvs[...]

    load_k.wait()
    load_v.wait()
    rest = pl.ds(0, block * (ranks - 1))
    for which, dest in ((0, kbuf), (1, vbuf)):
        pltpu.make_async_remote_copy(
            src_ref=dest.at[rest], dst_ref=dest.at[rest], send_sem=c_send.at[which], recv_sem=c_recv.at[which],
            device_id={"grp": sibling}, device_id_type=pl.DeviceIdType.MESH).wait()
    rest_q = pl.ds(0, 8 * (groups - 1))
    pltpu.make_async_remote_copy(
        src_ref=qs.at[rest_q], dst_ref=qr.at[rest_q], send_sem=q_sem.at[0], recv_sem=q_sem.at[1],
        device_id={"grp": sibling}, device_id_type=pl.DeviceIdType.MESH).wait()

    scale = 1.0 / math.sqrt(HD)
    tall = 8 * groups
    full = (groups, 8, HD)
    query = rotated(qr[...], jnp.broadcast_to(cos_q[None], full).reshape(tall, HD),
                    jnp.broadcast_to(sin_q[None], full).reshape(tall, HD)).astype(BF16)
    score = nt(query, kbuf[...])
    early = iota((1, block * ranks), 1) < prefix
    score = jnp.where(early, score * scale, NEGATIVE)
    top = jnp.max(score, axis=1, keepdims=True)
    weight = jnp.exp(score - top)
    total = jnp.sum(weight, axis=1, keepdims=True)
    mixed = nn(weight.astype(BF16), vbuf[...]) / total
    level = jnp.broadcast_to(top + jnp.log(total), (tall, HD))
    hi = level.astype(BF16).astype(F32)
    mid = (level - hi).astype(BF16).astype(F32)
    lo = level - hi - mid
    across = iota((tall, HD), 1)
    stats = jnp.where(across < 32, hi, jnp.where(across < 64, mid, lo))
    rs[...] = jnp.concatenate([mixed.reshape(full), stats.reshape(full)], axis=1).astype(BF16)

    def r_copy(step):
        other = lax.rem(g + step, groups)
        return pltpu.make_async_remote_copy(
            src_ref=rs.at[other], dst_ref=rr.at[g],
            send_sem=r_sem.at[0], recv_sem=r_sem.at[1],
            device_id={"grp": other}, device_id_type=pl.DeviceIdType.MESH)

    def send_r(step, carry):
        r_copy(step).start()
        return carry

    lax.fori_loop(1, groups, send_r, 0)
    rr[g] = rs[g]

    for step in (1, 2, 3):
        source = lax.rem(t + step, 4)
        pltpu.make_async_remote_copy(
            src_ref=kvs, dst_ref=kvx.at[source], send_sem=kv_send.at[step], recv_sem=kv_recv.at[source],
            device_id={"grp": sibling}, device_id_type=pl.DeviceIdType.MESH).wait_recv()
    wide = jnp.concatenate([kvx[0], kvx[1], kvx[2], kvx[3]], axis=1)
    a = iota((4 * HD, 2 * HD), 0)
    b = iota((4 * HD, 2 * HD), 1)
    lane_a = a & (HD - 1)
    goal = (lane_a >> 5) * HD + (a >> 7) * 32 + (lane_a & 31)
    spread = ((goal == b) & (lane_a < 64)).astype(F32).astype(BF16)
    both = nn(wide, spread)
    keys = rotated(both[:, :HD], cos_o, sin_o).astype(BF16)
    values = both[:, HD:].astype(BF16)
    same = (issue_d == issue_l[:, :rows]) & (pos_l[:, :rows] <= pos_d)
    own = []
    for head in range(2):
        mine = rotated(proj[:, head * HD:(head + 1) * HD].astype(F32), cos_o, sin_o).astype(BF16)
        part = jnp.where(same, nt(mine, keys) * scale, NEGATIVE)
        peak = jnp.max(part, axis=1, keepdims=True)
        share = jnp.where(same, jnp.exp(part - peak), 0.0)
        own.append((peak, jnp.sum(share, axis=1, keepdims=True), nn(share.astype(BF16), values)))

    big = 16 * groups
    r = iota((rows, big), 1)
    hit = (r >> 4) * CAP + (r & 3) == slot_d
    field = (r >> 2) & 3
    picks = [(hit & (field == kind)).astype(F32).astype(BF16) for kind in range(4)]

    rest_r = pl.ds(0, groups - 1)
    pltpu.make_async_remote_copy(
        src_ref=rs.at[rest_r], dst_ref=rr.at[rest_r], send_sem=r_sem.at[0], recv_sem=r_sem.at[1],
        device_id={"grp": sibling}, device_id_type=pl.DeviceIdType.MESH).wait()
    back = rr[...].reshape(big, HD)
    for head in range(2):
        cached = nn(picks[head], back)
        told = nn(picks[2 + head], back)
        log_c = told[:, 0:1] + told[:, 32:33] + told[:, 64:65]
        peak, total_o, mixed_o = own[head]
        summit = jnp.maximum(peak, log_c)
        part_o = jnp.exp(peak - summit)
        part_c = jnp.exp(log_c - summit)
        value = (mixed_o * part_o + cached * part_c) / (total_o * part_o + part_c)
        out_ref[:, head * HD:(head + 1) * HD] = value.astype(BF16)

    for copy in kv_copies:
        copy.wait_send()
    for copy in sends + hid_copies + [swap]:
        copy.wait_send()


def local(groups, ranks, hidden, w_proj, cache_keys, cache_values, cand_issue, cand_length, prefix_len):
    rows, model = hidden.shape
    depth, cols = w_proj.shape
    block = cache_keys.shape[1]
    spot = np.arange(HD) % (HD // 2)
    freq = np.broadcast_to((THETA ** (-2.0 * spot / HD)).astype(np.float32), (8, HD))
    any_space = pl.BlockSpec(memory_space=pl.ANY)
    smem = pl.BlockSpec(memory_space=pltpu.SMEM)
    vmem = pl.BlockSpec(memory_space=pltpu.VMEM)
    dma = pltpu.SemaphoreType.DMA
    return pl.pallas_call(
        functools.partial(kernel, groups, ranks),
        out_shape=jax.ShapeDtypeStruct((rows, 2 * HD), BF16),
        in_specs=[any_space] * 4 + [smem] * 3 + [vmem],
        out_specs=vmem,
        scratch_shapes=[
            pltpu.VMEM((2 * rows, model // 2), BF16),
            pltpu.VMEM((groups // 2, cols, depth), BF16),
            pltpu.VMEM((block * ranks, HD), BF16),
            pltpu.VMEM((block * ranks, HD), BF16),
            pltpu.VMEM((2 * rows, cols), F32),
            pltpu.VMEM((rows, cols), F32),
            pltpu.VMEM((8 * groups, HD), F32),
            pltpu.VMEM((8 * groups, HD), F32),
            pltpu.VMEM((rows, HD), BF16),
            pltpu.VMEM((4, rows, HD), BF16),
            pltpu.VMEM((groups, 16, HD), BF16),
            pltpu.VMEM((groups, 16, HD), BF16),
            dma((4,)), dma((20,)), dma((8,)), dma((9,)), dma((8,)), dma((8,)), dma((2,)), dma((2,)), dma((2,)), dma((2,)),
            dma((4,)), dma((4,)), dma((2,)),
        ],
        compiler_params=pltpu.CompilerParams(
            collective_id=0, has_side_effects=True, vmem_limit_bytes=60 * 1024 * 1024),
        cost_estimate=pl.CostEstimate(flops=10**9, bytes_accessed=2 * 10**6, transcendentals=10**6),
    )(hidden, w_proj.T, cache_keys, cache_values, cand_issue, cand_length, prefix_len, jnp.asarray(freq))


def solution(mesh):
    placed = (
        P("grp", None),
        P("grp", "tp"),
        P("grp", "tp", None),
        P("grp", "tp", None),
        P("grp"),
        P("grp"),
        P("grp"),
    )
    return jax.shard_map(
        functools.partial(local, mesh.shape["grp"], mesh.shape["tp"]),
        mesh=mesh, in_specs=placed, out_specs=P("grp", "tp"), check_vma=False)
```
